512 devices in a mesh: row: 32 (over y, x_hi, core), col: 16 (over z, x_lo).
Axes of the slice: x: 4 (x_hi: 2, x_lo: 2; x = x_hi * 2 + x_lo), y: 8, z: 8, core: 2. Of those that a mesh axis runs over, the one named last changes fastest.
Arguments:
- pair: float32 [256, 256, 128], P('row', 'col'), may hold values from -6 to 6
- pair_mask: int32 [256, 256], P('row', 'col'), may hold values 0 or 1
- w_project: bfloat16 [2, 128, 512], replicated, may hold values from -0.5 to 0.5
- w_gate: bfloat16 [2, 128, 128], replicated, may hold values from -0.5 to 0.5
- w_output: bfloat16 [2, 128, 128], replicated, may hold values from -0.5 to 0.5
Outputs:
- updated: float32 [256, 256, 128], P('row', 'col')
The draws below stay inside these ranges and needn't reach their ends.
All inputs are finite; a program needn't handle non-finite values. No bound on the sum of `pair_mask` on one device may be relied on, other than what follows from the above.
Results may differ from the reference program's by a relative error of at most 0.0046.
Values may be sent and summed in bfloat16 or wider, within the bound.
A program may use at most 64 MiB of HBM per device.

```python
import jax
import jax.numpy as jnp
from jax import lax

C = 128
H = 128
NRES = 256


def with_ends(drawn, rng, low, largest):
    spot = [jax.random.randint(jax.random.fold_in(rng, axis), (), 0, length) for axis, length in enumerate(drawn.shape)]
    main_axis = drawn.shape.index(max(drawn.shape))
    neighbour = spot[:main_axis] + [(spot[main_axis] + 1) % drawn.shape[main_axis]] + spot[main_axis + 1:]
    return drawn.at[tuple(spot)].set(low).at[tuple(neighbour)].set(largest)


def block_scale(key, shape, split, smallest, largest):
    gain, own = 1.0, jax.random.fold_in(key, 6)
    for dim, blocks in split:
        steps = jnp.exp(jax.random.uniform(jax.random.fold_in(own, dim), (blocks,), jnp.float32, smallest / len(split), largest / len(split)))
        gain = gain * jnp.repeat(steps, shape[dim] // blocks).reshape([-1 if axis == dim else 1 for axis in range(len(shape))])
    return gain


def scatter_about(stream_key, shape, width, bound, shards=(), held_as=jnp.bfloat16):
    gain = block_scale(stream_key, shape, shards, -0.22, 0.18) if shards else 1.0
    values = jax.random.normal(stream_key, shape, jnp.float32) * width * gain
    return jnp.minimum(jnp.maximum(values, -bound), bound).astype(held_as)


def setup_inputs(seed: int = 0) -> dict:
    seeds = jax.random.split(jax.random.key(seed), 6)
    return {
        "pair": scatter_about(seeds[0], (NRES, NRES, C), 1.0, 6.0, ((0, 32), (1, 16)), jnp.float32),
        "pair_mask": with_ends((jax.random.randint(seeds[1], (NRES, NRES), 0, 10) < 9).astype(jnp.int32), jax.random.fold_in(seeds[1], 1), 0, 1),
        "w_project": scatter_about(seeds[2], (2, C, 4 * H), C ** -0.5, 0.5),
        "w_gate": scatter_about(seeds[3], (2, C, C), C ** -0.5, 0.5),
        "w_output": scatter_about(seeds[4], (2, H, C), H ** -0.5, 0.5),
    }


def norm_last(values):
    center = values - lax.optimization_barrier(jnp.mean(values, axis=-1, keepdims=True))
    spread = lax.optimization_barrier(jnp.mean(center * center, axis=-1, keepdims=True))
    return center * lax.rsqrt(spread + 1e-05)

def one_update(state, mask_f, w_proj, w_gt, w_out, outgoing):
    normed = norm_last(state).astype(jnp.bfloat16)
    proj = jnp.einsum('ijc,cd->ijd', normed.astype(jnp.float32), w_proj.astype(jnp.float32), precision=lax.Precision.HIGHEST)
    weight = mask_f[..., None]
    left = (weight * jax.nn.sigmoid(proj[..., :H]) * proj[..., H:2 * H]).astype(jnp.bfloat16)
    right = (weight * jax.nn.sigmoid(proj[..., 2 * H:3 * H]) * proj[..., 3 * H:]).astype(jnp.bfloat16)
    gate = jax.nn.sigmoid(jnp.einsum('ijc,cd->ijd', normed.astype(jnp.float32), w_gt.astype(jnp.float32), precision=lax.Precision.HIGHEST))
    if outgoing:
        tri = jnp.einsum('ikh,jkh->ijh', left.astype(jnp.float32), right.astype(jnp.float32), precision=lax.Precision.HIGHEST)
    else:
        tri = jnp.einsum('kih,kjh->ijh', left.astype(jnp.float32), right.astype(jnp.float32), precision=lax.Precision.HIGHEST)
    tnorm = norm_last(tri).astype(jnp.bfloat16)
    result = jnp.einsum('ijh,hc->ijc', tnorm.astype(jnp.float32), w_out.astype(jnp.float32), precision=lax.Precision.HIGHEST)
    return state + gate * result

def reference(pair, pair_mask, w_project, w_gate, w_output):
    mask_f = pair_mask.astype(jnp.float32)
    state = one_update(pair, mask_f, w_project[0], w_gate[0], w_output[0], True)
    state = one_update(state, mask_f, w_project[1], w_gate[1], w_output[1], False)
    return state
```

```python
import functools

import jax
import jax.numpy as jnp
from jax import lax
from jax.experimental import pallas as pl
from jax.experimental.pallas import tpu as pltpu
from jax.sharding import PartitionSpec as P

MESH = pl.DeviceIdType.MESH
F32, BF16 = jnp.float32, jnp.bfloat16
GROUP, RING, BLOCK, SHARE = 8, 8, 32, 16
HALF = RING // 2


def coordinates():
    row, col = lax.axis_index("row"), lax.axis_index("col")
    x_hi, x_lo, core = (row // 2) % 2, col % 2, row % 2
    return (x_hi * 2 + x_lo) * 2 + core, row // 4, col // 2


def device(g, y, z):
    return ((y * 2 + g // 4) * 2 + g % 2, z * 2 + (g // 2) % 2)


def ahead(index, by):
    return lax.rem(index + by, 8)


def barrel(parts):
    block = lax.broadcasted_iota(jnp.int32, parts[0].shape, 1) // SHARE
    for bit in (1, 2, 4):
        odd = (block // bit) % 2 == 1
        parts = [jnp.where(odd, parts[(m + bit) % 8], parts[m]) for m in range(8)]
    return parts


def rolled(parts):
    return [parts[0]] + [pltpu.roll(parts[m], SHARE * m, 1) for m in range(1, 8)]


def swap_blocks(parts):
    out = barrel(rolled(barrel(parts)))
    return [out[-g % 8] for g in range(8)]


def fold_blocks(parts):
    turned = rolled(barrel(parts))
    while len(turned) > 1:
        turned = [a + b for a, b in zip(turned[::2], turned[1::2])]
    return turned[0]


def norm_last(values):
    center = values - jnp.mean(values, axis=-1, keepdims=True)
    spread = jnp.mean(center * center, axis=-1, keepdims=True)
    return center * lax.rsqrt(spread + 1e-05)


def operands(normed, weight, w_proj):
    proj = jnp.dot(normed, w_proj, preferred_element_type=F32)
    left = weight * jax.nn.sigmoid(proj[:, :128]) * proj[:, 128:256]
    right = weight * jax.nn.sigmoid(proj[:, 256:384]) * proj[:, 384:]
    return left, right


def kernel(pair, mask, w_project, w_gate, w_output, out, x, wp, wg, wo, mask_rows, gate, send_l, send_r, a_buf, b_buf, a_f, b_f, acc, t_send, t_buf, in_sem, s_sem, r_sem):
    g, y, z = coordinates()
    bar = pltpu.get_barrier_semaphore()
    turned = [(ahead(z, HALF), y), (z, ahead(y, HALF))]

    def signal(*who):
        pl.semaphore_signal(bar, inc=1, device_id=device(*who), device_id_type=MESH)

    loads = [
        pltpu.make_async_copy(source, target, in_sem.at[i])
        for i, (source, target) in enumerate([(pair, x), (w_project, wp), (w_gate, wg), (w_output, wo)])
    ]
    for load in loads:
        load.start()
    for d in range(8):
        for ty, tz in turned:
            signal(ahead(g, d), ty, tz)
    for d in range(1, 8):
        signal(g, y, ahead(z, d))
        signal(g, ahead(y, d), z)
        signal(ahead(g, d), y, z)

    def remote(u, n, source, target, who):
        return pltpu.make_async_remote_copy(
            src_ref=source, dst_ref=target, send_sem=s_sem.at[u, n], recv_sem=r_sem.at[u, n],
            device_id=device(*who), device_id_type=MESH,
        )

    def share_copy(u, d, sending):
        send, buf = (send_l, a_buf) if u == 0 else (send_r, b_buf)
        to = ahead(g, d)
        slot = g if sending else ahead(g, 8 - d)
        return remote(u, d - 1, send.at[u, to], buf.at[u, 0, slot], (to, y, z))

    def turn_copy(u, d, sending):
        send, buf = (send_r, b_buf) if u == 0 else (send_l, a_buf)
        to = ahead(g, d)
        slot = g if sending else ahead(g, 8 - d)
        return remote(u, 7 + d, send.at[u, to], buf.at[u, 0, slot], (to, *turned[u]))

    def z_copy(u, d, sending):
        return remote(u, 14 + d, a_buf.at[u, 0], a_buf.at[u, 8 - d], (g, y, ahead(z, d)))

    def y_copy(u, d, sending):
        return remote(u, 21 + d, b_buf.at[u, 0], b_buf.at[u, 8 - d], (g, ahead(y, d), z))

    def back_copy(u, d, sending):
        to = ahead(g, d)
        slot = g if sending else ahead(g, 8 - d)
        return remote(u, 28 + d, t_send.at[u, to], t_buf.at[u, slot], (to, y, z))

    FAR_FIRST = (4, 3, 5, 2, 6, 1, 7)

    def pack(u, left, right):
        both = jnp.concatenate([left.reshape(8, 16, 128), right.reshape(8, 16, 128)], axis=1)
        pieces = swap_blocks([both[k] for k in range(8)])
        for p in range(8):
            send_l[u, p] = pieces[p][:16].astype(BF16)
            send_r[u, p] = pieces[p][16:].astype(BF16)

    def exchange(u):
        for d in range(8):
            turn_copy(u, d, True).start()
        for d in range(1, 8):
            share_copy(u, d, True).start()
        stay, stay_buf = (send_l, a_buf) if u == 0 else (send_r, b_buf)
        stay_buf[u, 0, g] = stay[u, g]
        normed = norm_last(x[...]).astype(BF16)
        gate[...] = jax.nn.sigmoid(jnp.dot(normed, wg[u], preferred_element_type=F32))
        acc[...] = jnp.zeros_like(acc)
        stay_copy, cross_copy = (z_copy, y_copy) if u == 0 else (y_copy, z_copy)
        for d in range(1, 8):
            share_copy(u, d, False).wait_recv()
        for d in FAR_FIRST:
            stay_copy(u, d, True).start()
        for d in range(8):
            turn_copy(u, d, False).wait_recv()
        for d in FAR_FIRST:
            cross_copy(u, d, True).start()
        for d in range(1, 8):
            stay_copy(u, d, False).wait_recv()

    def widen(u, source, target):
        for p in range(8):
            x_hi, x_lo, core = p // 4, (p // 2) % 2, p % 2
            piece = source[p].astype(F32)
            if u == 0:
                first = (x_hi * 2 + core) * 8
                target[x_lo * 2, first : first + 8] = piece[:8]
                target[x_lo * 2 + 1, first : first + 8] = piece[8:]
            else:
                target[x_hi * 2 + core, x_lo * 16 : x_lo * 16 + 16] = piece

    def multiply(u):
        cross_sem0 = 21 if u == 0 else 14

        def block(t, _):
            odd = lax.rem(t, 2)
            cross = odd * ((t + 1) // 2) + (1 - odd) * lax.rem(8 - t // 2, 8)
            stay = lax.rem(cross + HALF + 8 + (y - z if u == 0 else z - y), 8)
            cross_buf = b_buf if u == 0 else a_buf

            @pl.when(t > 0)
            def _():
                n = cross_sem0 + 8 - cross
                remote(u, n, cross_buf.at[u, 0], cross_buf.at[u, cross], (g, y, z)).wait_recv()

            a_slot, b_slot = (stay, cross) if u == 0 else (cross, stay)
            widen(u, a_buf.at[u, a_slot], a_f)
            widen(u, b_buf.at[u, b_slot], b_f)

            def rows(c, _):
                total = [acc[c * 8 + i] for i in range(8)]
                for k in range(4):
                    b = b_f[k]
                    for i in range(8):
                        total[i] = total[i] + a_f[k, pl.ds(c * 8 + i, 1), :] * b
                for i in range(8):
                    acc[c * 8 + i] = total[i]
                return 0

            lax.fori_loop(0, 4, rows, 0)
            return 0

        lax.fori_loop(0, 8, block, 0)

    def give_back(u):
        def piece(d, _):
            to = ahead(g, 8 - d)
            row0, col0 = (to // 4 * 2 + to % 2) * 8, pl.multiple_of((to // 2) % 2 * 16, 16)
            t_send[u, to] = fold_blocks([acc[row0 + i, pl.ds(col0, 16), :] for i in range(8)])

            @pl.when(d < 8)
            def _():
                n = 28 + 8 - d
                remote(u, n, t_send.at[u, to], t_buf.at[u, g], (to, y, z)).start()

            return 0

        lax.fori_loop(1, 9, piece, 0)
        t_buf[u, g] = t_send[u, g]

    def finish(u):
        for d in range(1, 8):
            back_copy(u, d, False).wait_recv()
        tri = jnp.concatenate(swap_blocks([t_buf[u, p] for p in range(8)]), axis=0)
        tnorm = norm_last(tri).astype(BF16)
        result = jnp.dot(tnorm, wo[u], preferred_element_type=F32)
        return x[...] + gate[...] * result

    loads[0].wait()
    mask_f = mask[...].astype(F32)
    r = lax.broadcasted_iota(jnp.int32, (128, 128), 0)
    c = lax.broadcasted_iota(jnp.int32, (128, 128), 1)
    spread = jnp.concatenate([jnp.broadcast_to(mask_f[i : i + 1, :], (16, 16)) for i in range(8)], axis=0)
    picked = jnp.where(r[:, :16] % 16 == c[:, :16], spread, 0.0)
    mask_rows[...] = jnp.broadcast_to(jnp.sum(picked, axis=1, keepdims=True), (128, 128))

    columns = [x[pl.ds(k, 8, stride=16), :] for k in range(16)]
    weight = jnp.concatenate([jnp.broadcast_to(mask_f[:, k : k + 1], (8, 128)) for k in range(16)], axis=0)
    normed = norm_last(jnp.concatenate(columns, axis=0)).astype(BF16)
    loads[1].wait()
    left, right = operands(normed, weight, wp[0])
    order = lambda v: jnp.swapaxes(v.reshape(2, 8, 8, 128), 0, 1)
    pack(0, order(left), order(right))
    loads[2].wait()
    loads[3].wait()
    pl.semaphore_wait(bar, 16 + 21)
    exchange(0)
    multiply(0)
    give_back(0)
    x[...] = finish(0)

    normed = norm_last(x[...]).astype(BF16)
    left, right = operands(normed, mask_rows[...], wp[1])
    pack(1, left, right)
    exchange(1)
    multiply(1)
    give_back(1)
    out[...] = finish(1)

    for u in range(2):
        for d in range(8):
            turn_copy(u, d, True).wait_send()
        for d in range(1, 8):
            for copy in (share_copy, z_copy, y_copy, back_copy):
                copy(u, d, True).wait_send()


def per_device(pair, pair_mask, w_project, w_gate, w_output):
    any_space = pl.BlockSpec(memory_space=pl.ANY)
    vmem = pl.BlockSpec(memory_space=pltpu.VMEM)
    updated = pl.pallas_call(
        kernel,
        name="triangle",
        out_shape=jax.ShapeDtypeStruct((128, 128), F32),
        in_specs=[any_space, vmem, any_space, any_space, any_space],
        out_specs=vmem,
        scratch_shapes=[
            pltpu.VMEM((128, 128), F32),
            pltpu.VMEM((2, 128, 512), BF16),
            pltpu.VMEM((2, 128, 128), BF16),
            pltpu.VMEM((2, 128, 128), BF16),
            pltpu.VMEM((128, 128), F32),
            pltpu.VMEM((128, 128), F32),
            pltpu.VMEM((2, 8, 16, 128), BF16),
            pltpu.VMEM((2, 8, 16, 128), BF16),
            pltpu.VMEM((2, 8, 8, 16, 128), BF16),
            pltpu.VMEM((2, 8, 8, 16, 128), BF16),
            pltpu.VMEM((4, 32, 128), F32),
            pltpu.VMEM((4, 32, 128), F32),
            pltpu.VMEM((32, 32, 128), F32),
            pltpu.VMEM((2, 8, 16, 128), F32),
            pltpu.VMEM((2, 8, 16, 128), F32),
            pltpu.SemaphoreType.DMA((4,)),
            pltpu.SemaphoreType.DMA((2, 36)),
            pltpu.SemaphoreType.DMA((2, 36)),
        ],
        compiler_params=pltpu.CompilerParams(
            collective_id=0, has_side_effects=True, vmem_limit_bytes=32 * 1024 * 1024
        ),
    )(pair.reshape(128, 128), pair_mask, w_project, w_gate, w_output)
    return updated.reshape(pair.shape)


def solution(mesh):
    in_specs = (P("row", "col", None), P("row", "col"), P(), P(), P())
    return jax.shard_map(
        per_device, mesh=mesh, in_specs=in_specs, out_specs=P("row", "col", None), check_vma=False
    )
```

```python
import jax
import jax.numpy as jnp
from jax import lax
from jax.experimental import pallas as pl
from jax.experimental.pallas import tpu as pltpu
from jax.sharding import PartitionSpec as P

MESH = pl.DeviceIdType.MESH
F32, BF16 = jnp.float32, jnp.bfloat16
GROUP, RING, BLOCK, SHARE = 8, 8, 32, 16
HALF = RING // 2


def coordinates():
    row, col = lax.axis_index("row"), lax.axis_index("col")
    x_hi, x_lo, core = (row // 2) % 2, col % 2, row % 2
    return (x_hi * 2 + x_lo) * 2 + core, row // 4, col // 2


def device(g, y, z):
    return ((y * 2 + g // 4) * 2 + g % 2, z * 2 + (g // 2) % 2)


def ahead(index, by):
    return lax.rem(index + by, 8)


def partner(g, e):
    x_hi, x_lo, core = g // 4, (g // 2) % 2, g % 2
    return ((x_hi + e // 4) % 2 * 2 + (x_lo + e // 2) % 2) * 2 + (core + e) % 2


def barrel(parts):
    block = lax.broadcasted_iota(jnp.int32, parts[0].shape, 1) // SHARE
    for bit in (1, 2, 4):
        odd = (block // bit) % 2 == 1
        parts = [jnp.where(odd, parts[(m + bit) % 8], parts[m]) for m in range(8)]
    return parts


def rolled(parts):
    return [parts[0]] + [pltpu.roll(parts[m], SHARE * m, 1) for m in range(1, 8)]


def swap_blocks(parts):
    out = barrel(rolled(barrel(parts)))
    return [out[-g % 8] for g in range(8)]


def fold_blocks(parts):
    turned = rolled(barrel(parts))
    while len(turned) > 1:
        turned = [a + b for a, b in zip(turned[::2], turned[1::2])]
    return turned[0]


def norm_last(values):
    center = values - jnp.mean(values, axis=-1, keepdims=True)
    spread = jnp.mean(center * center, axis=-1, keepdims=True)
    return center * lax.rsqrt(spread + 1e-05)


def kernel(pair, mask, w_project, w_gate, w_output, out, x, mk, wp, wg, wo, mask_rows, gate, send_l, send_r, a_buf, b_buf, a_f, b_f, acc, t_send, t_buf, in_sem, s_sem, r_sem):
    g, y, z = coordinates()
    bar = pltpu.get_barrier_semaphore()
    turned = [(ahead(2 * y + HALF + 8, 8 - z), y), (z, ahead(2 * z + HALF + 8, 8 - y))]

    def signal(*who):
        pl.semaphore_signal(bar, inc=1, device_id=device(*who), device_id_type=MESH)

    loads = [
        pltpu.make_async_copy(source, target, in_sem.at[i])
        for i, (source, target) in enumerate(
            [(pair, x), (mask, mk), (w_project, wp), (w_gate, wg), (w_output, wo)]
        )
    ]
    for d in range(8):
        for ty, tz in turned:
            signal(ahead(g, d), ty, tz)
    for d in range(1, 8):
        signal(g, y, ahead(z, d))
        signal(g, ahead(y, d), z)
        signal(ahead(g, d), y, z)
    for load in loads:
        load.start()

    def remote(u, n, source, target, who):
        return pltpu.make_async_remote_copy(
            src_ref=source, dst_ref=target, send_sem=s_sem.at[u, n], recv_sem=r_sem.at[u, n],
            device_id=device(*who), device_id_type=MESH,
        )

    def stay_refs(u):
        return (send_l, a_buf) if u == 0 else (send_r, b_buf)

    def cross_refs(u):
        return (send_r, b_buf) if u == 0 else (send_l, a_buf)

    def share_copy(u, e, sending):
        send, buf = stay_refs(u)
        to = partner(g, e)
        return remote(u, e, send.at[u, to], buf.at[u, 0, g if sending else to], (to, y, z))

    def turn_copy(u, e, sending):
        send, buf = cross_refs(u)
        to = partner(g, e)
        return remote(u, 8 + e, send.at[u, to], buf.at[u, 0, g if sending else to], (to, *turned[u]))

    def z_copy(u, d, piece):
        return remote(u, 16 + d, a_buf.at[u, 0, piece], a_buf.at[u, 8 - d, piece], (g, y, ahead(z, d)))

    def y_copy(u, d, piece):
        return remote(u, 24 + d, b_buf.at[u, 0, piece], b_buf.at[u, 8 - d, piece], (g, ahead(y, d), z))

    def block_wait(u, first, buf, slot):
        remote(u, first + lax.rem(8 - slot, 8), buf.at[u, 0], buf.at[u, slot], (g, y, z)).wait_recv()

    def back_copy(u, e, sending):
        to = partner(g, e)
        return remote(u, 32 + e, t_send.at[u, to], t_buf.at[u, g if sending else to], (to, y, z))

    FAR_FIRST = (4, 3, 5, 2, 6, 1, 7)
    NEAR_FIRST = (0, 2, 6, 4, 1, 3, 7, 5)

    def pack(u, send, operand):
        pieces = swap_blocks([operand[k] for k in range(8)])
        for p in range(8):
            send[u, p] = pieces[p].astype(BF16)

    def send_cross(u):
        for e in reversed(NEAR_FIRST):
            turn_copy(u, e, True).start()

    def send_stay(u):
        for e in reversed(NEAR_FIRST[1:]):
            share_copy(u, e, True).start()
        send, buf = stay_refs(u)
        buf[u, 0, g] = send[u, g]

    def exchange(u):
        copy = z_copy if u == 0 else y_copy
        for e in NEAR_FIRST:
            if e:
                share_copy(u, e, False).wait_recv()
            for d in FAR_FIRST:
                copy(u, d, partner(g, e)).start()
        copy = y_copy if u == 0 else z_copy
        for e in NEAR_FIRST:
            turn_copy(u, e, False).wait_recv()
            for d in FAR_FIRST:
                copy(u, d, partner(g, e)).start()
        for d in range(1, 8):
            block_wait(u, 16 if u == 0 else 24, stay_refs(u)[1], d)

    def widen(u, source, target):
        for p in range(8):
            x_hi, x_lo, core = p // 4, (p // 2) % 2, p % 2
            piece = source[p].astype(F32)
            if u == 0:
                first = (x_hi * 2 + core) * 8
                target[x_lo * 2, first : first + 8] = piece[:8]
                target[x_lo * 2 + 1, first : first + 8] = piece[8:]
            else:
                target[x_hi * 2 + core, x_lo * 16 : x_lo * 16 + 16] = piece

    def multiply(u):
        def block(t, _):
            odd = lax.rem(t, 2)
            cross = odd * ((t + 1) // 2) + (1 - odd) * lax.rem(8 - t // 2, 8)
            stay = lax.rem(HALF + 16 - cross + (z - y if u == 0 else y - z), 8)

            @pl.when(t > 0)
            def _():
                block_wait(u, 24 if u == 0 else 16, cross_refs(u)[1], cross)

            a_slot, b_slot = (stay, cross) if u == 0 else (cross, stay)
            widen(u, a_buf.at[u, a_slot], a_f)
            widen(u, b_buf.at[u, b_slot], b_f)

            def rows(c, _):
                total = [acc[c * 8 + i] for i in range(8)]
                for k in range(4):
                    b = b_f[k]
                    for i in range(8):
                        total[i] = total[i] + a_f[k, pl.ds(c * 8 + i, 1), :] * b
                for i in range(8):
                    acc[c * 8 + i] = total[i]
                return 0

            lax.fori_loop(0, 4, rows, 0)
            return 0

        lax.fori_loop(0, 8, block, 0)

    def give_back(u):
        for e in reversed(NEAR_FIRST):
            to = partner(g, e)
            row0, col0 = (to // 4 * 2 + to % 2) * 8, pl.multiple_of((to // 2) % 2 * 16, 16)
            t_send[u, to] = fold_blocks([acc[row0 + i, pl.ds(col0, 16), :] for i in range(8)])
            if e:
                back_copy(u, e, True).start()
        t_buf[u, g] = t_send[u, g]

    def output_gate(u):
        normed = norm_last(x[...]).astype(BF16)
        gate[...] = jax.nn.sigmoid(jnp.dot(normed, wg[u], preferred_element_type=F32))
        acc[...] = jnp.zeros_like(acc)

    def finish(u):
        for e in range(1, 8):
            back_copy(u, e, False).wait_recv()
        tri = jnp.concatenate(swap_blocks([t_buf[u, p] for p in range(8)]), axis=0)
        tnorm = norm_last(tri).astype(BF16)
        result = jnp.dot(tnorm, wo[u], preferred_element_type=F32)
        return x[...] + gate[...] * result

    def operand(normed, weight, w_proj):
        proj = jnp.dot(normed, w_proj, preferred_element_type=F32)
        return weight * jax.nn.sigmoid(proj[:, :128]) * proj[:, 128:]

    loads[0].wait()
    columns = [x[pl.ds(k, 8, stride=16), :] for k in range(16)]
    normed = norm_last(jnp.concatenate(columns, axis=0)).astype(BF16)
    loads[1].wait()
    mask_f = mk[...].astype(F32)
    weight = jnp.concatenate([jnp.broadcast_to(mask_f[:, k : k + 1], (8, 128)) for k in range(16)], axis=0)
    loads[2].wait()

    def by_steps(v):
        return jnp.swapaxes(v.reshape(2, 8, 8, 128), 0, 1).reshape(8, 16, 128)

    pack(0, send_r, by_steps(operand(normed, weight, wp[0, :, 256:])))
    pack(0, send_l, by_steps(operand(normed, weight, wp[0, :, :256])))
    pl.semaphore_wait(bar, 16 + 21)
    send_cross(0)
    send_stay(0)
    loads[3].wait()
    loads[4].wait()
    output_gate(0)
    r = lax.broadcasted_iota(jnp.int32, (128, 16), 0)
    c = lax.broadcasted_iota(jnp.int32, (128, 16), 1)
    spread = jnp.concatenate([jnp.broadcast_to(mask_f[i : i + 1, :], (16, 16)) for i in range(8)], axis=0)
    picked = jnp.where(r % 16 == c, spread, 0.0)
    mask_rows[...] = jnp.broadcast_to(jnp.sum(picked, axis=1, keepdims=True), (128, 128))
    exchange(0)
    multiply(0)
    give_back(0)
    x[...] = finish(0)

    normed = norm_last(x[...]).astype(BF16)
    pack(1, send_l, operand(normed, mask_rows[...], wp[1, :, :256]).reshape(8, 16, 128))
    send_cross(1)
    pack(1, send_r, operand(normed, mask_rows[...], wp[1, :, 256:]).reshape(8, 16, 128))
    send_stay(1)
    output_gate(1)
    exchange(1)
    multiply(1)
    give_back(1)
    out[...] = finish(1)

    for u in range(2):
        for e in range(8):
            turn_copy(u, e, True).wait_send()
            if e:
                share_copy(u, e, True).wait_send()
                back_copy(u, e, True).wait_send()
        for d in range(1, 8):
            for n, buf in ((16, a_buf), (24, b_buf)):
                remote(u, n + d, buf.at[u, 0], buf.at[u, 0], (g, y, z)).wait_send()


def per_device(pair, pair_mask, w_project, w_gate, w_output):
    hbm = pl.BlockSpec(memory_space=pltpu.HBM)
    updated = pl.pallas_call(
        kernel,
        name="triangle",
        out_shape=jax.ShapeDtypeStruct((128, 128), F32),
        in_specs=[hbm] * 5,
        out_specs=pl.BlockSpec(memory_space=pltpu.VMEM),
        scratch_shapes=[
            pltpu.VMEM((128, 128), F32),
            pltpu.VMEM((8, 16), jnp.int32),
            pltpu.VMEM((2, 128, 512), BF16),
            pltpu.VMEM((2, 128, 128), BF16),
            pltpu.VMEM((2, 128, 128), BF16),
            pltpu.VMEM((128, 128), F32),
            pltpu.VMEM((128, 128), F32),
            pltpu.VMEM((2, 8, 16, 128), BF16),
            pltpu.VMEM((2, 8, 16, 128), BF16),
            pltpu.VMEM((2, 8, 8, 16, 128), BF16),
            pltpu.VMEM((2, 8, 8, 16, 128), BF16),
            pltpu.VMEM((4, 32, 128), F32),
            pltpu.VMEM((4, 32, 128), F32),
            pltpu.VMEM((32, 32, 128), F32),
            pltpu.VMEM((2, 8, 16, 128), F32),
            pltpu.VMEM((2, 8, 16, 128), F32),
            pltpu.SemaphoreType.DMA((5,)),
            pltpu.SemaphoreType.DMA((2, 40)),
            pltpu.SemaphoreType.DMA((2, 40)),
        ],
        compiler_params=pltpu.CompilerParams(
            collective_id=0, has_side_effects=True, vmem_limit_bytes=32 * 1024 * 1024
        ),
    )(*(pltpu.with_memory_space_constraint(v, pltpu.HBM) for v in (pair.reshape(128, 128), pair_mask, w_project, w_gate, w_output)))
    return updated.reshape(pair.shape)


def solution(mesh):
    in_specs = (P("row", "col", None), P("row", "col"), P(), P(), P())
    return jax.shard_map(
        per_device, mesh=mesh, in_specs=in_specs, out_specs=P("row", "col", None), check_vma=False
    )
```

```python
import jax
import jax.numpy as jnp
from jax import lax
from jax.experimental import pallas as pl
from jax.experimental.pallas import tpu as pltpu
from jax.sharding import PartitionSpec as P

MESH = pl.DeviceIdType.MESH
F32, BF16 = jnp.float32, jnp.bfloat16
GROUP, RING, SHARE = 4, 8, 32
HALF = RING // 2


def coordinates():
    row, col = lax.axis_index("row"), lax.axis_index("col")
    return (row // 2) % 2 * 2 + col % 2, row % 2, row // 4, col // 2


def device(x, core, y, z):
    return ((y * 2 + x // 2) * 2 + core, z * 2 + x % 2)


def ahead(index, by):
    return lax.rem(index + by, RING)


def partner(x, e):
    return (x // 2 + e // 2) % 2 * 2 + (x + e) % 2


def barrel(parts):
    block = lax.broadcasted_iota(jnp.int32, parts[0].shape, 1) // SHARE
    for bit in (1, 2):
        odd = (block // bit) % 2 == 1
        parts = [jnp.where(odd, parts[(m + bit) % GROUP], parts[m]) for m in range(GROUP)]
    return parts


def rolled(parts):
    return [parts[0]] + [pltpu.roll(parts[m], SHARE * m, 1) for m in range(1, GROUP)]


def swap_blocks(parts):
    out = barrel(rolled(barrel(parts)))
    return [out[-g % GROUP] for g in range(GROUP)]


def fold_blocks(parts):
    turned = rolled(barrel(parts))
    return (turned[0] + turned[1]) + (turned[2] + turned[3])


def norm_last(values):
    center = values - jnp.mean(values, axis=-1, keepdims=True)
    spread = jnp.mean(center * center, axis=-1, keepdims=True)
    return center * lax.rsqrt(spread + 1e-05)


FAR_FIRST = (4, 3, 5, 2, 6, 1, 7)
NEAR_FIRST = (0, 1, 3, 2)
STAY, CROSS, ALONG_Z, ALONG_Y, BACK, CHIP = 0, 4, 8, 16, 24, 32
MATES = ((2, 1), (3, 1), (1, 1), (2, 0), (3, 0), (1, 0), (0, 1))


def kernel(
    pair, mask, w_project, w_gate, w_output, out,
    state, mk, wp, wg, wo, mask_rows, gate, send_l, send_r, a_buf, b_buf, a_far, wide_stay0, wide_cross0, wide_stay1,
    wide_cross1, acc0, acc1, t_send0, t_send1, t_buf0, t_buf1, in_sem, s_sem, r_sem,
):
    x, core, y, z = coordinates()
    other = 1 - core
    bar = pltpu.get_barrier_semaphore()
    turned = [(ahead(2 * y + HALF + 8, 8 - z), y), (z, ahead(2 * z + HALF + 8, 8 - y))]

    def signal(*who):
        pl.semaphore_signal(bar, inc=1, device_id=device(*who), device_id_type=MESH)

    for e in range(GROUP):
        for ty, tz in turned:
            signal(partner(x, e), core, ty, tz)
    for d in range(1, RING):
        signal(x, core, y, ahead(z, d))
        signal(x, core, ahead(y, d), z)
    for e, c in MATES:
        signal(partner(x, e), (core + c) % 2, y, z)
    loads = [
        pltpu.make_async_copy(source, target, in_sem.at[i])
        for i, (source, target) in enumerate(
            [(pair, state), (mask, mk), (w_project, wp), (w_gate, wg), (w_output, wo)]
        )
    ]
    for load in loads:
        load.start()

    def remote(u, n, source, target, who):
        return pltpu.make_async_remote_copy(
            src_ref=source, dst_ref=target, send_sem=s_sem.at[u, n], recv_sem=r_sem.at[u, n],
            device_id=device(*who), device_id_type=MESH,
        )

    def stay_refs(u):
        return (send_l, a_buf) if u == 0 else (send_r, b_buf)

    def cross_refs(u):
        return (send_r, b_buf) if u == 0 else (send_l, a_buf)

    def share_copy(u, e, sending):
        send, buf = stay_refs(u)
        to = partner(x, e)
        return remote(u, STAY + e, send.at[u, to], buf.at[u, 0, x if sending else to], (to, core, y, z))

    def turn_copy(u, e, sending):
        send, buf = cross_refs(u)
        to = partner(x, e)
        return remote(u, CROSS + e, send.at[u, to], buf.at[u, 0, x if sending else to], (to, core, *turned[u]))

    def z_copy(u, d, piece):
        return remote(
            u, ALONG_Z + d, a_buf.at[u, 0, piece], a_buf.at[u, 8 - d, piece], (x, core, y, ahead(z, d))
        )

    def y_copy(u, d, piece):
        return remote(
            u, ALONG_Y + d, b_buf.at[u, 0, piece], b_buf.at[u, 8 - d, piece], (x, core, ahead(y, d), z)
        )

    def block_wait(u, first, buf, slot):
        remote(u, first + lax.rem(8 - slot, 8), buf.at[u, 0], buf.at[u, slot], (x, core, y, z)).wait_recv()

    def back_copy(u, e, c, sending):
        send, buf = (t_send0, t_buf0) if u == 0 else (t_send1, t_buf1)
        to, to_core = partner(x, e), (core + c) % 2
        slot = (x, core) if sending else (to, to_core)
        return remote(u, BACK + 2 * e + c, send.at[to, to_core], buf.at[slot], (to, to_core, y, z))

    def block_to_other(slot):
        return remote(0, CHIP + slot, a_buf.at[0, slot], a_far.at[slot], (x, other, y, z))

    def pack(u, send, operand):
        steps = operand.reshape(4, 4, 8, 128) if u == 0 else operand.reshape(2, 4, 16, 128)
        pieces = swap_blocks([steps[:, k].reshape(32, 128) for k in range(GROUP)])
        for p in range(GROUP):
            send[u, p] = pieces[p].astype(BF16)

    def send_cross(u):
        for e in reversed(NEAR_FIRST):
            turn_copy(u, e, True).start()

    def send_stay(u):
        for e in reversed(NEAR_FIRST[1:]):
            share_copy(u, e, True).start()
        send, buf = stay_refs(u)
        buf[u, 0, x] = send[u, x]

    def widen(u, source, target):
        for p in range(GROUP):
            x_hi, x_lo = p // 2, p % 2
            piece = source[p].astype(F32)
            if u == 0:
                target[x_lo * 4 : x_lo * 4 + 4, x_hi * 8 : x_hi * 8 + 8] = piece.reshape(4, 8, 128)
            else:
                target[x_hi * 2 : x_hi * 2 + 2, x_lo * 16 : x_lo * 16 + 16] = piece.reshape(2, 16, 128)

    def exchange(u):
        copy = z_copy if u == 0 else y_copy
        for e in NEAR_FIRST:
            if e:
                share_copy(u, e, False).wait_recv()
            for d in FAR_FIRST:
                copy(u, d, partner(x, e)).start()
        copy = y_copy if u == 0 else z_copy
        for e in NEAR_FIRST:
            turn_copy(u, e, False).wait_recv()
            for d in FAR_FIRST:
                copy(u, d, partner(x, e)).start()
        if u == 0:
            def arrive(slot, _):
                @pl.when(slot > 0)
                def _():
                    block_wait(0, ALONG_Z, a_buf, slot)

                block_to_other(slot).start()
                widen(0, a_buf.at[0, slot], wide_stay0.at[0, slot])
                return 0

            def arrive_other(slot, _):
                block_to_other(slot).wait_recv()
                widen(0, a_far.at[slot], wide_stay0.at[1, slot])
                return 0

            lax.fori_loop(0, 8, arrive, 0)
            lax.fori_loop(0, 8, arrive_other, 0)
        else:
            def arrive(slot, _):
                @pl.when(slot > 0)
                def _():
                    block_wait(1, ALONG_Y, b_buf, slot)

                widen(1, b_buf.at[1, slot], wide_stay1.at[slot])
                return 0

            lax.fori_loop(0, 8, arrive, 0)

    def nearest(t):
        odd = lax.rem(t, 2)
        return odd * ((t + 1) // 2) + (1 - odd) * lax.rem(8 - t // 2, 8)

    def stay_slot(u, cross):
        return lax.rem(HALF + 16 - cross + (z - y if u == 0 else y - z), 8)

    def multiply_first():
        def block(t, _):
            slot = nearest(t)

            @pl.when(t > 0)
            def _():
                block_wait(0, ALONG_Y, b_buf, slot)

            widen(0, b_buf.at[0, slot], wide_cross0)
            stay = stay_slot(0, slot)

            def rows(half, _):
                total = [acc0[half, i] for i in range(16)]
                for k in range(8):
                    b = wide_cross0[k]
                    for i in range(16):
                        total[i] = total[i] + wide_stay0[half, stay, k, pl.ds(i, 1), :] * b
                for i in range(16):
                    acc0[half, i] = total[i]
                return 0

            lax.fori_loop(0, 2, rows, 0)
            return 0

        lax.fori_loop(0, 8, block, 0)

    def multiply_second():
        def block(t, _):
            slot = nearest(t)

            @pl.when(t > 0)
            def _():
                block_wait(1, ALONG_Z, a_buf, slot)

            widen(1, a_buf.at[1, slot], wide_cross1)
            stay = stay_slot(1, slot)

            def rows(c, _):
                total = [acc1[c * 8 + i] for i in range(8)]
                for k in range(4):
                    b = wide_stay1[stay, k]
                    for i in range(8):
                        total[i] = total[i] + wide_cross1[k, pl.ds(c * 8 + i, 1), :] * b
                for i in range(8):
                    acc1[c * 8 + i] = total[i]
                return 0

            lax.fori_loop(0, 4, rows, 0)
            return 0

        lax.fori_loop(0, 8, block, 0)

    def give_back(u):
        def piece(to, c):
            if u == 0:
                columns = pl.ds(pl.multiple_of(to % 2 * 8, 8), 8)
                rows = [acc0[c, to // 2 * 8 + i, columns, :] for i in range(8)]
            else:
                columns = pl.ds(pl.multiple_of(to % 2 * 16, 16), 16)
                first = (to // 2 * 2 + (core + c) % 2) * 8
                rows = [acc1[first + i, columns, :] for i in range(8)]
            return jnp.concatenate([fold_blocks(rows[:GROUP]), fold_blocks(rows[GROUP:])], axis=0)

        send, buf = (t_send0, t_buf0) if u == 0 else (t_send1, t_buf1)
        for e, c in MATES:
            to = partner(x, e)
            send[to, (core + c) % 2] = piece(to, c)
            back_copy(u, e, c, True).start()
        buf[x, core] = piece(x, 0)

    def output_gate(u):
        normed = norm_last(state[...]).astype(BF16)
        gate[...] = jax.nn.sigmoid(jnp.dot(normed, wg[u], preferred_element_type=F32))
        acc = acc0 if u == 0 else acc1
        acc[...] = jnp.zeros_like(acc)

    def finish(u):
        for e, c in MATES:
            back_copy(u, e, c, False).wait_recv()
        if u == 0:
            parts = [
                jnp.stack([t_buf0[p, c].reshape(2, 8, 128) for c in range(2)], axis=1).reshape(32, 128)
                for p in range(GROUP)
            ]
        else:
            parts = [t_buf1[p, 0] + t_buf1[p, 1] for p in range(GROUP)]
        parts = swap_blocks(parts)
        tri = jnp.stack([part.reshape(2, 16, 128) for part in parts], axis=1).reshape(128, 128)
        tnorm = norm_last(tri).astype(BF16)
        result = jnp.dot(tnorm, wo[u], preferred_element_type=F32)
        return state[...] + gate[...] * result

    def operand(normed, weight, w_proj):
        proj = jnp.dot(normed, w_proj, preferred_element_type=F32)
        return weight * jax.nn.sigmoid(proj[:, :128]) * proj[:, 128:]

    loads[0].wait()
    columns = [state[pl.ds(k, 8, stride=16), :] for k in range(16)]
    normed = norm_last(jnp.concatenate(columns, axis=0)).astype(BF16)
    loads[1].wait()
    mask_f = mk[...].astype(F32)
    weight = jnp.concatenate([jnp.broadcast_to(mask_f[:, k : k + 1], (8, 128)) for k in range(16)], axis=0)
    loads[2].wait()
    pack(0, send_r, operand(normed, weight, wp[0, :, 256:]))
    pack(0, send_l, operand(normed, weight, wp[0, :, :256]))
    pl.semaphore_wait(bar, 2 * GROUP + 2 * (RING - 1) + len(MATES))
    send_cross(0)
    send_stay(0)
    loads[3].wait()
    loads[4].wait()
    output_gate(0)
    r = lax.broadcasted_iota(jnp.int32, (128, 16), 0)
    c = lax.broadcasted_iota(jnp.int32, (128, 16), 1)
    spread = jnp.concatenate([jnp.broadcast_to(mask_f[i : i + 1, :], (16, 16)) for i in range(8)], axis=0)
    picked = jnp.where(r % 16 == c, spread, 0.0)
    mask_rows[...] = jnp.broadcast_to(jnp.sum(picked, axis=1, keepdims=True), (128, 128))
    exchange(0)
    multiply_first()
    give_back(0)
    state[...] = finish(0)

    normed = norm_last(state[...]).astype(BF16)
    pack(1, send_l, operand(normed, mask_rows[...], wp[1, :, :256]))
    send_cross(1)
    pack(1, send_r, operand(normed, mask_rows[...], wp[1, :, 256:]))
    send_stay(1)
    output_gate(1)
    exchange(1)
    multiply_second()
    give_back(1)
    out[...] = finish(1)

    for u in range(2):
        for e in range(GROUP):
            turn_copy(u, e, True).wait_send()
            if e:
                share_copy(u, e, True).wait_send()
        for e, c in MATES:
            back_copy(u, e, c, True).wait_send()
        for d in range(1, RING):
            for n, buf in ((ALONG_Z, a_buf), (ALONG_Y, b_buf)):
                remote(u, n + d, buf.at[u, 0], buf.at[u, 0], (x, core, y, z)).wait_send()
    for slot in range(RING):
        block_to_other(slot).wait_send()


def per_device(pair, pair_mask, w_project, w_gate, w_output):
    hbm = pl.BlockSpec(memory_space=pltpu.HBM)
    operands = (pair.reshape(128, 128), pair_mask, w_project, w_gate, w_output)
    updated = pl.pallas_call(
        kernel,
        name="triangle",
        out_shape=jax.ShapeDtypeStruct((128, 128), F32),
        in_specs=[hbm] * 5,
        out_specs=pl.BlockSpec(memory_space=pltpu.VMEM),
        scratch_shapes=[
            pltpu.VMEM((128, 128), F32),
            pltpu.VMEM((8, 16), jnp.int32),
            pltpu.VMEM((2, 128, 512), BF16),
            pltpu.VMEM((2, 128, 128), BF16),
            pltpu.VMEM((2, 128, 128), BF16),
            pltpu.VMEM((128, 128), F32),
            pltpu.VMEM((128, 128), F32),
            pltpu.VMEM((2, 4, 32, 128), BF16),
            pltpu.VMEM((2, 4, 32, 128), BF16),
            pltpu.VMEM((2, 8, 4, 32, 128), BF16),
            pltpu.VMEM((2, 8, 4, 32, 128), BF16),
            pltpu.VMEM((8, 4, 32, 128), BF16),
            pltpu.VMEM((2, 8, 8, 16, 128), F32),
            pltpu.VMEM((8, 16, 128), F32),
            pltpu.VMEM((8, 4, 32, 128), F32),
            pltpu.VMEM((4, 32, 128), F32),
            pltpu.VMEM((2, 16, 16, 128), F32),
            pltpu.VMEM((32, 32, 128), F32),
            pltpu.VMEM((4, 2, 16, 128), F32),
            pltpu.VMEM((4, 2, 32, 128), F32),
            pltpu.VMEM((4, 2, 16, 128), F32),
            pltpu.VMEM((4, 2, 32, 128), F32),
            pltpu.SemaphoreType.DMA((5,)),
            pltpu.SemaphoreType.DMA((2, 40)),
            pltpu.SemaphoreType.DMA((2, 40)),
        ],
        compiler_params=pltpu.CompilerParams(
            collective_id=0, has_side_effects=True, vmem_limit_bytes=32 * 1024 * 1024
        ),
    )(*(pltpu.with_memory_space_constraint(value, pltpu.HBM) for value in operands))
    return updated.reshape(pair.shape)


def solution(mesh):
    in_specs = (P("row", "col", None), P("row", "col"), P(), P(), P())
    return jax.shard_map(
        per_device, mesh=mesh, in_specs=in_specs, out_specs=P("row", "col", None), check_vma=False
    )
```

```python
import jax
import jax.numpy as jnp
from jax import lax
from jax.experimental import pallas as pl
from jax.experimental.pallas import tpu as pltpu
from jax.sharding import PartitionSpec as P

MESH = pl.DeviceIdType.MESH
F32, BF16 = jnp.float32, jnp.bfloat16
GROUP, RING, SHARE = 4, 8, 32
HALF = RING // 2


def coordinates():
    row, col = lax.axis_index("row"), lax.axis_index("col")
    return (row // 2) % 2 * 2 + col % 2, row % 2, row // 4, col // 2


def device(x, core, y, z):
    return ((y * 2 + x // 2) * 2 + core, z * 2 + x % 2)


def ahead(index, by):
    return lax.rem(index + by, RING)


def partner(x, e):
    return (x // 2 + e // 2) % 2 * 2 + (x + e) % 2


def barrel(parts):
    block = lax.broadcasted_iota(jnp.int32, parts[0].shape, 1) // SHARE
    for bit in (1, 2):
        odd = (block // bit) % 2 == 1
        parts = [jnp.where(odd, parts[(m + bit) % GROUP], parts[m]) for m in range(GROUP)]
    return parts


def rolled(parts):
    return [parts[0]] + [pltpu.roll(parts[m], SHARE * m, 1) for m in range(1, GROUP)]


def swap_blocks(parts):
    out = barrel(rolled(barrel(parts)))
    return [out[-g % GROUP] for g in range(GROUP)]


def fold_blocks(parts):
    turned = rolled(barrel(parts))
    return (turned[0] + turned[1]) + (turned[2] + turned[3])


def norm_last(values):
    center = values - jnp.mean(values, axis=-1, keepdims=True)
    spread = jnp.mean(center * center, axis=-1, keepdims=True)
    return center * lax.rsqrt(spread + 1e-05)


FAR_FIRST = (4, 3, 5, 2, 6, 1, 7)
NEAR_FIRST = (0, 1, 3, 2)
STAY, CROSS, ALONG_Z, ALONG_Y, BACK, CHIP = 0, 4, 8, 16, 24, 32
MATES = ((2, 1), (3, 1), (1, 1), (2, 0), (3, 0), (1, 0), (0, 1))


def kernel(
    pair, mask, w_project, w_gate, w_output, out,
    state, mk, wp, wg, wo, mask_rows, gate, send_l, send_r, a_buf, b_buf, a_far, wide_stay0, wide_cross0, wide_stay1,
    wide_cross1, acc0, acc1, t_send0, t_send1, t_buf0, t_buf1, in_sem, s_sem, r_sem,
):
    x, core, y, z = coordinates()
    other = 1 - core
    bar = pltpu.get_barrier_semaphore()
    turned = [(ahead(2 * y + HALF + 8, 8 - z), y), (z, ahead(y, HALF))]
    sources = [(z, ahead(2 * z + HALF + 8, 8 - y)), (ahead(z, HALF), y)]

    def signal(*who):
        pl.semaphore_signal(bar, inc=1, device_id=device(*who), device_id_type=MESH)

    for e in range(GROUP):
        for ty, tz in sources:
            signal(partner(x, e), core, ty, tz)
    for d in range(1, RING):
        signal(x, core, y, ahead(z, d))
        signal(x, core, ahead(y, d), z)
    for e, c in MATES:
        signal(partner(x, e), (core + c) % 2, y, z)
    loads = [
        pltpu.make_async_copy(source, target, in_sem.at[i])
        for i, (source, target) in enumerate(
            [(pair, state), (mask, mk), (w_project, wp), (w_gate, wg), (w_output, wo)]
        )
    ]
    for load in loads:
        load.start()

    def remote(u, n, source, target, who):
        return pltpu.make_async_remote_copy(
            src_ref=source, dst_ref=target, send_sem=s_sem.at[u, n], recv_sem=r_sem.at[u, n],
            device_id=device(*who), device_id_type=MESH,
        )

    def stay_refs(u):
        return (send_l, a_buf) if u == 0 else (send_r, b_buf)

    def cross_refs(u):
        return (send_r, b_buf) if u == 0 else (send_l, a_buf)

    def share_copy(u, e, sending):
        send, buf = stay_refs(u)
        to = partner(x, e)
        return remote(u, STAY + e, send.at[u, to], buf.at[u, 0, x if sending else to], (to, core, y, z))

    def turn_copy(u, e, sending):
        send, buf = cross_refs(u)
        to = partner(x, e)
        return remote(u, CROSS + e, send.at[u, to], buf.at[u, 0, x if sending else to], (to, core, *turned[u]))

    def z_copy(u, d, piece):
        return remote(
            u, ALONG_Z + d, a_buf.at[u, 0, piece], a_buf.at[u, 8 - d, piece], (x, core, y, ahead(z, d))
        )

    def y_copy(u, d, piece):
        return remote(
            u, ALONG_Y + d, b_buf.at[u, 0, piece], b_buf.at[u, 8 - d, piece], (x, core, ahead(y, d), z)
        )

    def block_wait(u, first, buf, slot):
        remote(u, first + lax.rem(8 - slot, 8), buf.at[u, 0], buf.at[u, slot], (x, core, y, z)).wait_recv()

    def back_copy(u, e, c, sending):
        send, buf = (t_send0, t_buf0) if u == 0 else (t_send1, t_buf1)
        to, to_core = partner(x, e), (core + c) % 2
        slot = (x, core) if sending else (to, to_core)
        return remote(u, BACK + 2 * e + c, send.at[to, to_core], buf.at[slot], (to, to_core, y, z))

    def block_to_other(slot):
        return remote(0, CHIP + slot, a_buf.at[0, slot], a_far.at[slot], (x, other, y, z))

    def pack(u, send, operand):
        steps = operand.reshape(4, 4, 8, 128) if u == 0 else operand.reshape(2, 4, 16, 128)
        pieces = swap_blocks([steps[:, k].reshape(32, 128) for k in range(GROUP)])
        for p in range(GROUP):
            send[u, p] = pieces[p].astype(BF16)

    def send_cross(u):
        for e in reversed(NEAR_FIRST):
            turn_copy(u, e, True).start()

    def send_stay(u):
        for e in reversed(NEAR_FIRST[1:]):
            share_copy(u, e, True).start()
        send, buf = stay_refs(u)
        buf[u, 0, x] = send[u, x]

    def widen(u, source, target):
        for p in range(GROUP):
            x_hi, x_lo = p // 2, p % 2
            piece = source[p].astype(F32)
            if u == 0:
                target[x_lo * 4 : x_lo * 4 + 4, x_hi * 8 : x_hi * 8 + 8] = piece.reshape(4, 8, 128)
            else:
                target[x_hi * 2 : x_hi * 2 + 2, x_lo * 16 : x_lo * 16 + 16] = piece.reshape(2, 16, 128)

    def exchange(u):
        copy = z_copy if u == 0 else y_copy
        for e in NEAR_FIRST:
            if e:
                share_copy(u, e, False).wait_recv()
            for d in FAR_FIRST:
                copy(u, d, partner(x, e)).start()
        copy = y_copy if u == 0 else z_copy
        for e in NEAR_FIRST:
            turn_copy(u, e, False).wait_recv()
            for d in FAR_FIRST:
                copy(u, d, partner(x, e)).start()
        if u == 0:
            def arrive(slot, _):
                @pl.when(slot > 0)
                def _():
                    block_wait(0, ALONG_Z, a_buf, slot)

                block_to_other(slot).start()
                widen(0, a_buf.at[0, slot], wide_stay0.at[0, slot])
                return 0

            def arrive_other(slot, _):
                block_to_other(slot).wait_recv()
                widen(0, a_far.at[slot], wide_stay0.at[1, slot])
                return 0

            lax.fori_loop(0, 8, arrive, 0)
            lax.fori_loop(0, 8, arrive_other, 0)
        else:
            def arrive(slot, _):
                @pl.when(slot > 0)
                def _():
                    block_wait(1, ALONG_Y, b_buf, slot)

                widen(1, b_buf.at[1, slot], wide_stay1.at[slot])
                return 0

            lax.fori_loop(0, 8, arrive, 0)

    def nearest(t):
        odd = lax.rem(t, 2)
        return odd * ((t + 1) // 2) + (1 - odd) * lax.rem(8 - t // 2, 8)

    def stay_slot(u, cross):
        if u == 1:
            return lax.rem(HALF + 8 + cross + z - y, 8)
        return lax.rem(HALF + 16 - cross + z - y, 8)

    def multiply_first():
        def block(t, _):
            slot = nearest(t)

            @pl.when(t > 0)
            def _():
                block_wait(0, ALONG_Y, b_buf, slot)

            widen(0, b_buf.at[0, slot], wide_cross0)
            stay = stay_slot(0, slot)

            def rows(half, _):
                total = [acc0[half, i] for i in range(16)]
                for k in range(8):
                    b = wide_cross0[k]
                    for i in range(16):
                        total[i] = total[i] + wide_stay0[half, stay, k, pl.ds(i, 1), :] * b
                for i in range(16):
                    acc0[half, i] = total[i]
                return 0

            lax.fori_loop(0, 2, rows, 0)
            return 0

        lax.fori_loop(0, 8, block, 0)

    def multiply_second():
        def block(t, _):
            slot = nearest(t)

            @pl.when(t > 0)
            def _():
                block_wait(1, ALONG_Z, a_buf, slot)

            widen(1, a_buf.at[1, slot], wide_cross1)
            stay = stay_slot(1, slot)

            def rows(c, _):
                total = [acc1[c * 8 + i] for i in range(8)]
                for k in range(4):
                    b = wide_stay1[stay, k]
                    for i in range(8):
                        total[i] = total[i] + wide_cross1[k, pl.ds(c * 8 + i, 1), :] * b
                for i in range(8):
                    acc1[c * 8 + i] = total[i]
                return 0

            lax.fori_loop(0, 4, rows, 0)
            return 0

        lax.fori_loop(0, 8, block, 0)

    def give_back(u):
        def piece(to, c):
            if u == 0:
                columns = pl.ds(pl.multiple_of(to % 2 * 8, 8), 8)
                rows = [acc0[c, to // 2 * 8 + i, columns, :] for i in range(8)]
            else:
                columns = pl.ds(pl.multiple_of(to % 2 * 16, 16), 16)
                first = (to // 2 * 2 + (core + c) % 2) * 8
                rows = [acc1[first + i, columns, :] for i in range(8)]
            return jnp.concatenate([fold_blocks(rows[:GROUP]), fold_blocks(rows[GROUP:])], axis=0)

        send, buf = (t_send0, t_buf0) if u == 0 else (t_send1, t_buf1)
        for e, c in MATES:
            to = partner(x, e)
            send[to, (core + c) % 2] = piece(to, c)
            back_copy(u, e, c, True).start()
        buf[x, core] = piece(x, 0)

    def output_gate(u):
        normed = norm_last(state[...]).astype(BF16)
        gate[...] = jax.nn.sigmoid(jnp.dot(normed, wg[u], preferred_element_type=F32))
        acc = acc0 if u == 0 else acc1
        acc[...] = jnp.zeros_like(acc)

    def finish(u):
        for e, c in MATES:
            back_copy(u, e, c, False).wait_recv()
        if u == 0:
            parts = [
                jnp.stack([t_buf0[p, c].reshape(2, 8, 128) for c in range(2)], axis=1).reshape(32, 128)
                for p in range(GROUP)
            ]
        else:
            parts = [t_buf1[p, 0] + t_buf1[p, 1] for p in range(GROUP)]
        parts = swap_blocks(parts)
        tri = jnp.stack([part.reshape(2, 16, 128) for part in parts], axis=1).reshape(128, 128)
        tnorm = norm_last(tri).astype(BF16)
        result = jnp.dot(tnorm, wo[u], preferred_element_type=F32)
        return state[...] + gate[...] * result

    def operand(normed, weight, w_proj):
        proj = jnp.dot(normed, w_proj, preferred_element_type=F32)
        return weight * jax.nn.sigmoid(proj[:, :128]) * proj[:, 128:]

    def sent(u):
        for e in range(GROUP):
            turn_copy(u, e, True).wait_send()
            if e:
                share_copy(u, e, True).wait_send()
        for e, c in MATES:
            back_copy(u, e, c, True).wait_send()
        for d in range(1, RING):
            for n, buf in ((ALONG_Z, a_buf), (ALONG_Y, b_buf)):
                remote(u, n + d, buf.at[u, 0], buf.at[u, 0], (x, core, y, z)).wait_send()
        if u == 0:
            for slot in range(RING):
                block_to_other(slot).wait_send()

    loads[0].wait()
    columns = [state[pl.ds(k, 8, stride=16), :] for k in range(16)]
    normed = norm_last(jnp.concatenate(columns, axis=0)).astype(BF16)
    loads[1].wait()
    mask_f = mk[...].astype(F32)
    weight = jnp.concatenate([jnp.broadcast_to(mask_f[:, k : k + 1], (8, 128)) for k in range(16)], axis=0)
    loads[2].wait()
    pack(0, send_r, operand(normed, weight, wp[0, :, 256:]))
    pack(0, send_l, operand(normed, weight, wp[0, :, :256]))
    pl.semaphore_wait(bar, 2 * GROUP + 2 * (RING - 1) + len(MATES))
    send_cross(0)
    send_stay(0)
    loads[3].wait()
    loads[4].wait()
    output_gate(0)
    r = lax.broadcasted_iota(jnp.int32, (128, 16), 0)
    c = lax.broadcasted_iota(jnp.int32, (128, 16), 1)
    spread = jnp.concatenate([jnp.broadcast_to(mask_f[i : i + 1, :], (16, 16)) for i in range(8)], axis=0)
    picked = jnp.where(r % 16 == c, spread, 0.0)
    mask_rows[...] = jnp.broadcast_to(jnp.sum(picked, axis=1, keepdims=True), (128, 128))
    exchange(0)
    multiply_first()
    give_back(0)
    state[...] = finish(0)

    normed = norm_last(state[...]).astype(BF16)
    pack(1, send_l, operand(normed, mask_rows[...], wp[1, :, :256]))
    send_cross(1)
    pack(1, send_r, operand(normed, mask_rows[...], wp[1, :, 256:]))
    send_stay(1)
    output_gate(1)
    sent(0)
    exchange(1)
    multiply_second()
    give_back(1)
    sent(1)
    out[...] = finish(1)


def per_device(pair, pair_mask, w_project, w_gate, w_output):
    hbm = pl.BlockSpec(memory_space=pltpu.HBM)
    operands = (pair.reshape(128, 128), pair_mask, w_project, w_gate, w_output)
    updated = pl.pallas_call(
        kernel,
        name="triangle",
        out_shape=jax.ShapeDtypeStruct((128, 128), F32),
        in_specs=[hbm] * 5,
        out_specs=pl.BlockSpec(memory_space=pltpu.VMEM),
        scratch_shapes=[
            pltpu.VMEM((128, 128), F32),
            pltpu.VMEM((8, 16), jnp.int32),
            pltpu.VMEM((2, 128, 512), BF16),
            pltpu.VMEM((2, 128, 128), BF16),
            pltpu.VMEM((2, 128, 128), BF16),
            pltpu.VMEM((128, 128), F32),
            pltpu.VMEM((128, 128), F32),
            pltpu.VMEM((2, 4, 32, 128), BF16),
            pltpu.VMEM((2, 4, 32, 128), BF16),
            pltpu.VMEM((2, 8, 4, 32, 128), BF16),
            pltpu.VMEM((2, 8, 4, 32, 128), BF16),
            pltpu.VMEM((8, 4, 32, 128), BF16),
            pltpu.VMEM((2, 8, 8, 16, 128), F32),
            pltpu.VMEM((8, 16, 128), F32),
            pltpu.VMEM((8, 4, 32, 128), F32),
            pltpu.VMEM((4, 32, 128), F32),
            pltpu.VMEM((2, 16, 16, 128), F32),
            pltpu.VMEM((32, 32, 128), F32),
            pltpu.VMEM((4, 2, 16, 128), F32),
            pltpu.VMEM((4, 2, 32, 128), F32),
            pltpu.VMEM((4, 2, 16, 128), F32),
            pltpu.VMEM((4, 2, 32, 128), F32),
            pltpu.SemaphoreType.DMA((5,)),
            pltpu.SemaphoreType.DMA((2, 40)),
            pltpu.SemaphoreType.DMA((2, 40)),
        ],
        compiler_params=pltpu.CompilerParams(
            collective_id=0, has_side_effects=True, vmem_limit_bytes=32 * 1024 * 1024
        ),
    )(*(pltpu.with_memory_space_constraint(value, pltpu.HBM) for value in operands))
    return updated.reshape(pair.shape)


def solution(mesh):
    in_specs = (P("row", "col", None), P("row", "col"), P(), P(), P())
    return jax.shard_map(
        per_device, mesh=mesh, in_specs=in_specs, out_specs=P("row", "col", None), check_vma=False
    )
```

```python
import jax
import jax.numpy as jnp
from jax import lax
from jax.experimental import pallas as pl
from jax.experimental.pallas import tpu as pltpu
from jax.sharding import PartitionSpec as P

MESH = pl.DeviceIdType.MESH
F32, BF16 = jnp.float32, jnp.bfloat16
GROUP, RING, SHARE = 4, 8, 32
HALF = RING // 2


def coordinates():
    row, col = lax.axis_index("row"), lax.axis_index("col")
    return (row // 2) % 2 * 2 + col % 2, row % 2, row // 4, col // 2


def device(x, core, y, z):
    return ((y * 2 + x // 2) * 2 + core, z * 2 + x % 2)


def ahead(index, by):
    return lax.rem(index + by, RING)


def partner(x, e):
    return (x // 2 + e // 2) % 2 * 2 + (x + e) % 2


def barrel(parts):
    block = lax.broadcasted_iota(jnp.int32, parts[0].shape, 1) // SHARE
    for bit in (1, 2):
        odd = (block // bit) % 2 == 1
        parts = [jnp.where(odd, parts[(m + bit) % GROUP], parts[m]) for m in range(GROUP)]
    return parts


def rolled(parts):
    return [parts[0]] + [pltpu.roll(parts[m], SHARE * m, 1) for m in range(1, GROUP)]


def swap_blocks(parts):
    out = barrel(rolled(barrel(parts)))
    return [out[-g % GROUP] for g in range(GROUP)]


def fold_blocks(parts):
    turned = rolled(barrel(parts))
    return (turned[0] + turned[1]) + (turned[2] + turned[3])


def norm_last(values):
    center = values - jnp.mean(values, axis=-1, keepdims=True)
    spread = jnp.mean(center * center, axis=-1, keepdims=True)
    return center * lax.rsqrt(spread + 1e-05)


FAR_FIRST = (4, 3, 5, 2, 6, 1, 7)
NEAR_FIRST = (0, 1, 3, 2)
STAY, CROSS, ALONG_Z, ALONG_Y, BACK, CHIP = 0, 4, 8, 16, 24, 32
MATES = ((2, 1), (3, 1), (1, 1), (2, 0), (3, 0), (1, 0), (0, 1))


def kernel(
    pair, mask, w_project, w_gate, w_output, out,
    state, mk, wp, wg, wo, mask_rows, gate, send_l, send_r, a_buf, b_buf, a_far, wide_stay0, wide_cross0, wide_stay1,
    wide_cross1, acc0, acc1, t_send0, t_send1, t_buf0, t_buf1, in_sem, s_sem, r_sem,
):
    x, core, y, z = coordinates()
    other = 1 - core
    bar = pltpu.get_barrier_semaphore()
    turned = [(ahead(2 * y + HALF + 8, 8 - z), y), (z, ahead(y, HALF))]
    sources = [(z, ahead(2 * z + HALF + 8, 8 - y)), (ahead(z, HALF), y)]

    def signal(*who):
        pl.semaphore_signal(bar, inc=1, device_id=device(*who), device_id_type=MESH)

    for e in range(GROUP):
        for ty, tz in sources:
            signal(partner(x, e), core, ty, tz)
    for d in range(1, RING):
        signal(x, core, y, ahead(z, d))
        signal(x, core, ahead(y, d), z)
    for e, c in MATES:
        signal(partner(x, e), (core + c) % 2, y, z)
    loads = [
        pltpu.make_async_copy(source, target, in_sem.at[i])
        for i, (source, target) in enumerate(
            [(pair, state), (mask, mk), (w_project, wp), (w_gate, wg), (w_output, wo)]
        )
    ]
    for load in loads:
        load.start()

    def remote(u, n, source, target, who):
        return pltpu.make_async_remote_copy(
            src_ref=source, dst_ref=target, send_sem=s_sem.at[u, n], recv_sem=r_sem.at[u, n],
            device_id=device(*who), device_id_type=MESH,
        )

    def stay_refs(u):
        return (send_l, a_buf) if u == 0 else (send_r, b_buf)

    def cross_refs(u):
        return (send_r, b_buf) if u == 0 else (send_l, a_buf)

    def share_copy(u, e, sending):
        send, buf = stay_refs(u)
        to = partner(x, e)
        return remote(u, STAY + e, send.at[u, to], buf.at[u, 0, x if sending else to], (to, core, y, z))

    def turn_copy(u, e, sending):
        send, buf = cross_refs(u)
        to = partner(x, e)
        return remote(u, CROSS + e, send.at[u, to], buf.at[u, 0, x if sending else to], (to, core, *turned[u]))

    def z_copy(u, d, piece):
        return remote(
            u, ALONG_Z + d, a_buf.at[u, 0, piece], a_buf.at[u, 8 - d, piece], (x, core, y, ahead(z, d))
        )

    def y_copy(u, d, piece):
        return remote(
            u, ALONG_Y + d, b_buf.at[u, 0, piece], b_buf.at[u, 8 - d, piece], (x, core, ahead(y, d), z)
        )

    def block_wait(u, first, buf, slot):
        remote(u, first + lax.rem(8 - slot, 8), buf.at[u, 0], buf.at[u, slot], (x, core, y, z)).wait_recv()

    def back_copy(u, e, c, sending):
        send, buf = (t_send0, t_buf0) if u == 0 else (t_send1, t_buf1)
        to, to_core = partner(x, e), (core + c) % 2
        slot = (x, core) if sending else (to, to_core)
        return remote(u, BACK + 2 * e + c, send.at[to, to_core], buf.at[slot], (to, to_core, y, z))

    def block_to_other(slot):
        return remote(0, CHIP + slot, a_buf.at[0, slot], a_far.at[slot], (x, other, y, z))

    def pack(u, send, operand):
        steps = operand.reshape(4, 4, 8, 128) if u == 0 else operand.reshape(2, 4, 16, 128)
        pieces = swap_blocks([steps[:, k].reshape(32, 128) for k in range(GROUP)])
        for p in range(GROUP):
            send[u, p] = pieces[p].astype(BF16)

    def send_cross(u):
        for e in reversed(NEAR_FIRST):
            turn_copy(u, e, True).start()

    def send_stay(u):
        for e in reversed(NEAR_FIRST[1:]):
            share_copy(u, e, True).start()
        send, buf = stay_refs(u)
        buf[u, 0, x] = send[u, x]

    def widen(u, source, target):
        for p in range(GROUP):
            x_hi, x_lo = p // 2, p % 2
            piece = source[p].astype(F32)
            if u == 0:
                target[x_lo * 4 : x_lo * 4 + 4, x_hi * 8 : x_hi * 8 + 8] = piece.reshape(4, 8, 128)
            else:
                target[x_hi * 2 : x_hi * 2 + 2, x_lo * 16 : x_lo * 16 + 16] = piece.reshape(2, 16, 128)

    def both(e):
        return pl.ds(partner(x, e) // 2 * 2, 2)

    def exchange(u):
        copy = z_copy if u == 0 else y_copy
        for pair in (NEAR_FIRST[:2], NEAR_FIRST[2:]):
            for e in pair:
                if e:
                    share_copy(u, e, False).wait_recv()
            for d in FAR_FIRST:
                copy(u, d, both(pair[0])).start()
        copy = y_copy if u == 0 else z_copy
        for e in NEAR_FIRST:
            turn_copy(u, e, False).wait_recv()
            for d in FAR_FIRST:
                copy(u, d, partner(x, e)).start()
        if u == 0:
            def arrive(slot, _):
                @pl.when(slot > 0)
                def _():
                    block_wait(0, ALONG_Z, a_buf, slot)

                block_to_other(slot).start()
                widen(0, a_buf.at[0, slot], wide_stay0.at[0, slot])
                return 0

            def arrive_other(slot, _):
                block_to_other(slot).wait_recv()
                widen(0, a_far.at[slot], wide_stay0.at[1, slot])
                return 0

            lax.fori_loop(0, 8, arrive, 0)
            lax.fori_loop(0, 8, arrive_other, 0)
        else:
            def arrive(slot, _):
                @pl.when(slot > 0)
                def _():
                    block_wait(1, ALONG_Y, b_buf, slot)

                widen(1, b_buf.at[1, slot], wide_stay1.at[slot])
                return 0

            lax.fori_loop(0, 8, arrive, 0)

    def nearest(t):
        odd = lax.rem(t, 2)
        return odd * ((t + 1) // 2) + (1 - odd) * lax.rem(8 - t // 2, 8)

    def stay_slot(u, cross):
        if u == 1:
            return lax.rem(HALF + 8 + cross + z - y, 8)
        return lax.rem(HALF + 16 - cross + z - y, 8)

    def multiply_first():
        def block(t, _):
            slot = nearest(t)

            @pl.when(t > 0)
            def _():
                block_wait(0, ALONG_Y, b_buf, slot)

            widen(0, b_buf.at[0, slot], wide_cross0)
            stay = stay_slot(0, slot)

            def rows(half, _):
                total = [acc0[half, i] for i in range(16)]
                for k in range(8):
                    b = wide_cross0[k]
                    for i in range(16):
                        total[i] = total[i] + wide_stay0[half, stay, k, pl.ds(i, 1), :] * b
                for i in range(16):
                    acc0[half, i] = total[i]
                return 0

            lax.fori_loop(0, 2, rows, 0)
            return 0

        lax.fori_loop(0, 8, block, 0)

    def multiply_second():
        def block(t, _):
            slot = nearest(t)

            @pl.when(t > 0)
            def _():
                block_wait(1, ALONG_Z, a_buf, slot)

            widen(1, a_buf.at[1, slot], wide_cross1)
            stay = stay_slot(1, slot)

            def rows(c, _):
                total = [acc1[c * 8 + i] for i in range(8)]
                for k in range(4):
                    b = wide_stay1[stay, k]
                    for i in range(8):
                        total[i] = total[i] + wide_cross1[k, pl.ds(c * 8 + i, 1), :] * b
                for i in range(8):
                    acc1[c * 8 + i] = total[i]
                return 0

            lax.fori_loop(0, 4, rows, 0)
            return 0

        lax.fori_loop(0, 8, block, 0)

    def give_back(u):
        def piece(to, c):
            if u == 0:
                columns = pl.ds(pl.multiple_of(to % 2 * 8, 8), 8)
                rows = [acc0[c, to // 2 * 8 + i, columns, :] for i in range(8)]
            else:
                columns = pl.ds(pl.multiple_of(to % 2 * 16, 16), 16)
                first = (to // 2 * 2 + (core + c) % 2) * 8
                rows = [acc1[first + i, columns, :] for i in range(8)]
            return jnp.concatenate([fold_blocks(rows[:GROUP]), fold_blocks(rows[GROUP:])], axis=0)

        send, buf = (t_send0, t_buf0) if u == 0 else (t_send1, t_buf1)
        for e, c in MATES:
            to = partner(x, e)
            send[to, (core + c) % 2] = piece(to, c)
            back_copy(u, e, c, True).start()
        buf[x, core] = piece(x, 0)

    def output_gate(u):
        normed = norm_last(state[...]).astype(BF16)
        gate[...] = jax.nn.sigmoid(jnp.dot(normed, wg[u], preferred_element_type=F32))
        acc = acc0 if u == 0 else acc1
        acc[...] = jnp.zeros_like(acc)

    def finish(u):
        for e, c in MATES:
            back_copy(u, e, c, False).wait_recv()
        if u == 0:
            parts = [
                jnp.stack([t_buf0[p, c].reshape(2, 8, 128) for c in range(2)], axis=1).reshape(32, 128)
                for p in range(GROUP)
            ]
        else:
            parts = [t_buf1[p, 0] + t_buf1[p, 1] for p in range(GROUP)]
        parts = swap_blocks(parts)
        tri = jnp.stack([part.reshape(2, 16, 128) for part in parts], axis=1).reshape(128, 128)
        tnorm = norm_last(tri).astype(BF16)
        result = jnp.dot(tnorm, wo[u], preferred_element_type=F32)
        return state[...] + gate[...] * result

    def operand(normed, weight, w_proj):
        proj = jnp.dot(normed, w_proj, preferred_element_type=F32)
        return weight * jax.nn.sigmoid(proj[:, :128]) * proj[:, 128:]

    def sent(u):
        for e in range(GROUP):
            turn_copy(u, e, True).wait_send()
            if e:
                share_copy(u, e, True).wait_send()
        for e, c in MATES:
            back_copy(u, e, c, True).wait_send()
        for d in range(1, RING):
            for n, buf in ((ALONG_Z, a_buf), (ALONG_Y, b_buf)):
                remote(u, n + d, buf.at[u, 0], buf.at[u, 0], (x, core, y, z)).wait_send()
        if u == 0:
            for slot in range(RING):
                block_to_other(slot).wait_send()

    loads[0].wait()
    columns = [state[pl.ds(k, 8, stride=16), :] for k in range(16)]
    normed = norm_last(jnp.concatenate(columns, axis=0)).astype(BF16)
    loads[1].wait()
    mask_f = mk[...].astype(F32)
    weight = jnp.concatenate([jnp.broadcast_to(mask_f[:, k : k + 1], (8, 128)) for k in range(16)], axis=0)
    loads[2].wait()
    pack(0, send_r, operand(normed, weight, wp[0, :, 256:]))
    pack(0, send_l, operand(normed, weight, wp[0, :, :256]))
    pl.semaphore_wait(bar, 2 * GROUP + 2 * (RING - 1) + len(MATES))
    send_cross(0)
    send_stay(0)
    loads[3].wait()
    loads[4].wait()
    output_gate(0)
    r = lax.broadcasted_iota(jnp.int32, (128, 16), 0)
    c = lax.broadcasted_iota(jnp.int32, (128, 16), 1)
    spread = jnp.concatenate([jnp.broadcast_to(mask_f[i : i + 1, :], (16, 16)) for i in range(8)], axis=0)
    picked = jnp.where(r % 16 == c, spread, 0.0)
    mask_rows[...] = jnp.broadcast_to(jnp.sum(picked, axis=1, keepdims=True), (128, 128))
    exchange(0)
    multiply_first()
    give_back(0)
    state[...] = finish(0)

    normed = norm_last(state[...]).astype(BF16)
    pack(1, send_l, operand(normed, mask_rows[...], wp[1, :, :256]))
    send_cross(1)
    pack(1, send_r, operand(normed, mask_rows[...], wp[1, :, 256:]))
    send_stay(1)
    output_gate(1)
    sent(0)
    exchange(1)
    multiply_second()
    give_back(1)
    sent(1)
    out[...] = finish(1)


def per_device(pair, pair_mask, w_project, w_gate, w_output):
    hbm = pl.BlockSpec(memory_space=pltpu.HBM)
    operands = (pair.reshape(128, 128), pair_mask, w_project, w_gate, w_output)
    updated = pl.pallas_call(
        kernel,
        name="triangle",
        out_shape=jax.ShapeDtypeStruct((128, 128), F32),
        in_specs=[hbm] * 5,
        out_specs=pl.BlockSpec(memory_space=pltpu.VMEM),
        scratch_shapes=[
            pltpu.VMEM((128, 128), F32),
            pltpu.VMEM((8, 16), jnp.int32),
            pltpu.VMEM((2, 128, 512), BF16),
            pltpu.VMEM((2, 128, 128), BF16),
            pltpu.VMEM((2, 128, 128), BF16),
            pltpu.VMEM((128, 128), F32),
            pltpu.VMEM((128, 128), F32),
            pltpu.VMEM((2, 4, 32, 128), BF16),
            pltpu.VMEM((2, 4, 32, 128), BF16),
            pltpu.VMEM((2, 8, 4, 32, 128), BF16),
            pltpu.VMEM((2, 8, 4, 32, 128), BF16),
            pltpu.VMEM((8, 4, 32, 128), BF16),
            pltpu.VMEM((2, 8, 8, 16, 128), F32),
            pltpu.VMEM((8, 16, 128), F32),
            pltpu.VMEM((8, 4, 32, 128), F32),
            pltpu.VMEM((4, 32, 128), F32),
            pltpu.VMEM((2, 16, 16, 128), F32),
            pltpu.VMEM((32, 32, 128), F32),
            pltpu.VMEM((4, 2, 16, 128), F32),
            pltpu.VMEM((4, 2, 32, 128), F32),
            pltpu.VMEM((4, 2, 16, 128), F32),
            pltpu.VMEM((4, 2, 32, 128), F32),
            pltpu.SemaphoreType.DMA((5,)),
            pltpu.SemaphoreType.DMA((2, 40)),
            pltpu.SemaphoreType.DMA((2, 40)),
        ],
        compiler_params=pltpu.CompilerParams(
            collective_id=0, has_side_effects=True, vmem_limit_bytes=32 * 1024 * 1024
        ),
    )(*(pltpu.with_memory_space_constraint(value, pltpu.HBM) for value in operands))
    return updated.reshape(pair.shape)


def solution(mesh):
    in_specs = (P("row", "col", None), P("row", "col"), P(), P(), P())
    return jax.shard_map(
        per_device, mesh=mesh, in_specs=in_specs, out_specs=P("row", "col", None), check_vma=False
    )
```
